32 devices in a mesh: groups: 2 (over x), section: 16 (over z, y, core).
Axes of the slice: x: 2, y: 2, z: 4, core: 2. Of those that a mesh axis runs over, the one named last changes fastest.
Arguments:
- query_grads: bfloat16 [512, 8192], P(('groups', 'section')), parts along dimension 0, may hold values from -8 to 8
- key_vals: bfloat16 [4096, 8192], P(('groups', 'section')), parts along dimension 0, may hold values from -8 to 8
Outputs:
- target_out: bfloat16 [512, 8192], P(('groups', 'section')), parts along dimension 0
- source_grads: bfloat16 [4096, 8192], P(('groups', 'section')), parts along dimension 0
The draws below stay inside these ranges and needn't reach their ends.
There are 2 independent parts, one for each index of `groups`. The reference program is written for one: setup_inputs(seed, part) draws one part's arguments, and reference() takes and returns one part's arrays. A program takes and returns all parts, laid end to end along the dimension named above; each array names one. Nothing has to cross between parts.
All inputs are finite; a program needn't handle non-finite values.
Results may differ from the reference program's by a relative error of at most 0.0052.
Values may be sent and summed in bfloat16 or wider, within the bound.
A program may use at most 128 MiB of HBM per device.

```python
import jax
import jax.numpy as jnp
from jax import lax

HEADS = 64
HEAD = 64
TGT = 256
SRC = 2048


def base_pairs(key, rows, salt):
    inner = jax.random.fold_in(key, salt)
    return jnp.clip(jax.random.normal(inner, (rows, HEADS, 2, HEAD), jnp.float32), -5.0, 5.0)


def draw_query_grads(key, part):
    values = base_pairs(key, TGT, 11)
    return values.reshape(TGT, 2 * HEADS * HEAD).astype(jnp.bfloat16)


def draw_key_vals(key, part):
    values = base_pairs(key, SRC, 23)
    return values.reshape(SRC, 2 * HEADS * HEAD).astype(jnp.bfloat16)


def setup_inputs(seed: int = 0, part: int = 0) -> dict:
    arg_keys = jax.random.split(jax.random.key(seed), 3)
    part_keys = jax.random.split(jax.random.fold_in(arg_keys[2], part), 3)
    return {
        "query_grads": draw_query_grads(jax.random.fold_in(jax.random.fold_in(arg_keys[2], part), 71), part),
        "key_vals": draw_key_vals(jax.random.fold_in(jax.random.fold_in(arg_keys[2], part), 71), part),
    }


def reference(query_grads, key_vals):
    score_scale = HEAD ** -0.5
    target_pairs = jnp.moveaxis(query_grads.reshape(TGT, HEADS, 2, HEAD), 1, 0)
    source_pairs = jnp.moveaxis(key_vals.reshape(SRC, HEADS, 2, HEAD), 1, 0)

    def per_head(operands):
        tpair, spair = operands
        query = tpair[:, 0]
        dctx = tpair[:, 1]
        keys = spair[:, 0]
        vals = spair[:, 1]
        scores = jnp.dot(query, keys.T, preferred_element_type=jnp.float32) * score_scale
        probs = jax.nn.softmax(scores, axis=-1)
        probs_low = probs.astype(jnp.bfloat16)
        context = jnp.dot(probs_low, vals, preferred_element_type=jnp.float32).astype(jnp.bfloat16)
        d_probs = jnp.dot(dctx, vals.T, preferred_element_type=jnp.float32)
        d_scores = (probs * (d_probs - jnp.sum(probs * d_probs, axis=-1, keepdims=True)) * score_scale).astype(jnp.bfloat16)
        d_query = jnp.dot(d_scores, keys, preferred_element_type=jnp.float32).astype(jnp.bfloat16)
        d_keys = jnp.dot(d_scores.T, query, preferred_element_type=jnp.float32).astype(jnp.bfloat16)
        d_vals = jnp.dot(probs_low.T, dctx, preferred_element_type=jnp.float32).astype(jnp.bfloat16)
        return jnp.stack([context, d_query], axis=1), jnp.stack([d_keys, d_vals], axis=1)

    target_heads, source_heads = lax.map(per_head, (target_pairs, source_pairs))
    target_out = jnp.moveaxis(target_heads, 0, 1).reshape(TGT, 2 * HEADS * HEAD)
    source_grads = jnp.moveaxis(source_heads, 0, 1).reshape(SRC, 2 * HEADS * HEAD)
    return target_out, source_grads
```

```python
import math

import jax
import jax.numpy as jnp
from jax import lax
from jax.experimental import pallas as pl
from jax.experimental.pallas import tpu as pltpu
from jax.sharding import PartitionSpec as P

HEAD = 64
PAIR = 2 * HEAD
CHUNKS = 1


def dot(a, b, da, db):
    return lax.dot_general(
        a, b, (((da,), (db,)), ((), ())), preferred_element_type=jnp.float32
    )


def attend(scale, step, qd_ref, kv_ref, out_ref, sg_ref, s_scr, dp_scr, acc):
    sources = kv_ref.shape[0]
    targets = qd_ref.shape[0]
    steps = sources // step
    block = pl.program_id(1)
    blocks = pl.num_programs(1)
    qd = qd_ref[...]
    lane = lax.broadcasted_iota(jnp.int32, (step, PAIR), 1)
    first = lane < HEAD
    zero = jnp.zeros((step, PAIR), jnp.bfloat16)
    low = jnp.full((8, targets), -jnp.inf, jnp.float32)

    peak = low
    for i in range(steps):
        rows = pl.ds(i * step, step)
        kv = kv_ref[rows, :]
        s = dot(jnp.where(first, kv, zero), qd, 1, 1) * scale
        s_scr[rows, :] = s
        dp_scr[rows, :] = dot(jnp.where(first, zero, kv), qd, 1, 1)
        peak = jnp.maximum(peak, jnp.max(s.reshape(step // 8, 8, targets), axis=0))
    peak = jnp.max(peak, axis=0, keepdims=True)

    total = jnp.zeros((8, targets), jnp.float32)
    mixed = jnp.zeros((8, targets), jnp.float32)
    for i in range(steps):
        rows = pl.ds(i * step, step)
        e = jnp.exp(s_scr[rows, :] - peak)
        s_scr[rows, :] = e
        total = total + jnp.sum(e.reshape(step // 8, 8, targets), axis=0)
        mixed = mixed + jnp.sum((e * dp_scr[rows, :]).reshape(step // 8, 8, targets), axis=0)
    inverse = 1.0 / jnp.sum(total, axis=0, keepdims=True)
    shift = jnp.sum(mixed, axis=0, keepdims=True) * inverse

    out = jnp.zeros((targets, PAIR), jnp.float32)
    for i in range(steps):
        rows = pl.ds(i * step, step)
        probs = s_scr[rows, :] * inverse
        probs_low = probs.astype(jnp.bfloat16)
        d_scores = (probs * (dp_scr[rows, :] - shift) * scale).astype(jnp.bfloat16)
        kv = kv_ref[rows, :]
        vk = jnp.concatenate([kv[:, HEAD:], kv[:, :HEAD]], axis=1)
        out = out + dot(probs_low, jnp.where(first, vk, zero), 0, 0)
        out = out + dot(d_scores, jnp.where(first, zero, vk), 0, 0)
        grads = jnp.where(first, dot(d_scores, qd, 1, 0), dot(probs_low, qd, 1, 0))
        if acc is None:
            sg_ref[rows, :] = grads.astype(jnp.bfloat16)
        else:
            prior = jnp.where(block == 0, 0.0, acc[rows, :])
            grads = prior + grads
            acc[rows, :] = grads

            @pl.when(block == blocks - 1)
            def _():
                sg_ref[rows, :] = grads.astype(jnp.bfloat16)

    out_ref[...] = out.astype(jnp.bfloat16)


def attention(qd, kv):
    targets, columns = qd.shape
    sources = kv.shape[0]
    heads = columns // PAIR
    tile = math.gcd(targets, 256)
    step = math.gcd(sources, 256)
    scale = HEAD ** (-0.5)
    single = targets == tile
    scratch = [
        pltpu.VMEM((sources, tile), jnp.float32),
        pltpu.VMEM((sources, tile), jnp.float32),
    ]
    if single:
        def body(*refs):
            attend(scale, step, *refs, None)
    else:
        scratch.append(pltpu.VMEM((sources, PAIR), jnp.float32))

        def body(*refs):
            attend(scale, step, *refs)

    return pl.pallas_call(
        body,
        grid=(heads, targets // tile),
        out_shape=(
            jax.ShapeDtypeStruct((targets, columns), jnp.bfloat16),
            jax.ShapeDtypeStruct((sources, columns), jnp.bfloat16),
        ),
        in_specs=[
            pl.BlockSpec((tile, PAIR), lambda h, t: (t, h)),
            pl.BlockSpec((sources, PAIR), lambda h, t: (0, h)),
        ],
        out_specs=(
            pl.BlockSpec((tile, PAIR), lambda h, t: (t, h)),
            pl.BlockSpec((sources, PAIR), lambda h, t: (0, h)),
        ),
        scratch_shapes=scratch,
        compiler_params=pltpu.CompilerParams(vmem_limit_bytes=48 * 1024 * 1024),
        cost_estimate=pl.CostEstimate(
            flops=24 * targets * sources * PAIR * heads,
            bytes_accessed=4 * (targets + sources) * columns,
            transcendentals=targets * sources * heads,
        ),
        name="attention",
    )(qd, kv)


def to_heads(x):
    return lax.all_to_all(x, "section", split_axis=1, concat_axis=0, tiled=True)


def to_rows(x):
    return lax.all_to_all(x, "section", split_axis=0, concat_axis=1, tiled=True)


def solution(mesh):
    devices = mesh.shape["section"]

    def per_device(query_grads, key_vals):
        columns = query_grads.shape[1]
        chunks = math.gcd(CHUNKS, columns // (PAIR * devices))
        width = columns // chunks
        outs, grads = [], []
        for c in range(chunks):
            part = slice(c * width, (c + 1) * width)
            qd = to_heads(query_grads[:, part])
            kv = to_heads(key_vals[:, part])
            out, grad = attention(qd, kv)
            outs.append(to_rows(out))
            grads.append(to_rows(grad))
        return jnp.concatenate(outs, axis=1), jnp.concatenate(grads, axis=1)

    return jax.shard_map(
        per_device,
        mesh=mesh,
        in_specs=(P(("groups", "section"), None), P(("groups", "section"), None)),
        out_specs=(P(("groups", "section"), None), P(("groups", "section"), None)),
        check_vma=False,
    )
```

```python
import functools
import math

import jax
import jax.numpy as jnp
from jax import lax
from jax.experimental import pallas as pl
from jax.experimental.pallas import tpu as pltpu
from jax.sharding import PartitionSpec as P

HEAD = 64
PAIR = 2 * HEAD


def dot(a, b, da, db):
    return lax.dot_general(
        a, b, (((da,), (db,)), ((), ())), preferred_element_type=jnp.float32
    )


def attend(h, tile, step, qd_all, kv_all, out_all, sg_all, s_scr, dp_scr, acc):
    scale = HEAD ** (-0.5)
    sources = kv_all.shape[1]
    targets = qd_all.shape[1]
    tiles = targets // tile
    steps = sources // step
    first = lax.broadcasted_iota(jnp.int32, (step, PAIR), 1) < HEAD
    zero = jnp.zeros((step, PAIR), jnp.bfloat16)

    for t in range(tiles):
        qd = qd_all[h, pl.ds(t * tile, tile), :]
        peak = jnp.full((8, tile), -jnp.inf, jnp.float32)
        for i in range(steps):
            rows = pl.ds(i * step, step)
            kv = kv_all[h, rows, :]
            s = dot(jnp.where(first, kv, zero), qd, 1, 1) * scale
            s_scr[rows, :] = s
            dp_scr[rows, :] = dot(jnp.where(first, zero, kv), qd, 1, 1)
            peak = jnp.maximum(peak, jnp.max(s.reshape(step // 8, 8, tile), axis=0))
        peak = jnp.max(peak, axis=0, keepdims=True)

        total = jnp.zeros((8, tile), jnp.float32)
        mixed = jnp.zeros((8, tile), jnp.float32)
        for i in range(steps):
            rows = pl.ds(i * step, step)
            e = jnp.exp(s_scr[rows, :] - peak)
            s_scr[rows, :] = e
            total = total + jnp.sum(e.reshape(step // 8, 8, tile), axis=0)
            mixed = mixed + jnp.sum((e * dp_scr[rows, :]).reshape(step // 8, 8, tile), axis=0)
        inverse = 1.0 / jnp.sum(total, axis=0, keepdims=True)
        shift = jnp.sum(mixed, axis=0, keepdims=True) * inverse

        out = jnp.zeros((tile, PAIR), jnp.float32)
        for i in range(steps):
            rows = pl.ds(i * step, step)
            probs = s_scr[rows, :] * inverse
            probs_low = probs.astype(jnp.bfloat16)
            d_scores = (probs * (dp_scr[rows, :] - shift) * scale).astype(jnp.bfloat16)
            kv = kv_all[h, rows, :]
            vk = jnp.concatenate([kv[:, HEAD:], kv[:, :HEAD]], axis=1)
            out = out + dot(probs_low, jnp.where(first, vk, zero), 0, 0)
            out = out + dot(d_scores, jnp.where(first, zero, vk), 0, 0)
            grads = jnp.where(first, dot(d_scores, qd, 1, 0), dot(probs_low, qd, 1, 0))
            if t > 0:
                grads = acc[rows, :] + grads
            if t < tiles - 1:
                acc[rows, :] = grads
            else:
                sg_all[h, rows, :] = grads.astype(jnp.bfloat16)
        out_all[h, pl.ds(t * tile, tile), :] = out.astype(jnp.bfloat16)


def kernel(
    n, heads, tile, step,
    qg, kvs, to, sg,
    qd_all, kv_all, out_all, sg_all, s_scr, dp_scr, acc,
    q_send, q_recv, k_send, k_recv, o_send, o_recv, g_send, g_recv, own,
):
    me = lax.axis_index("section")
    t_rows = qg.shape[0]
    s_rows = kvs.shape[0]

    def partner(d):
        return lax.rem(me + d, n)

    def rows_of(p, rows):
        return pl.ds(pl.multiple_of(p * rows, rows), rows)

    def cols_of(p, h):
        return pl.ds(pl.multiple_of((p * heads + h) * PAIR, PAIR), PAIR)

    def push(src, dst, send, recv, p):
        return pltpu.make_async_remote_copy(
            src_ref=src, dst_ref=dst, send_sem=send, recv_sem=recv,
            device_id={"section": p}, device_id_type=pl.DeviceIdType.MESH,
        )

    def q_copy(h, p, w):
        return push(qg.at[:, cols_of(p, h)], qd_all.at[h, rows_of(w, t_rows), :],
                    q_send.at[h, p], q_recv.at[h, w], p)

    def k_copy(h, p, w):
        return push(kvs.at[:, cols_of(p, h)], kv_all.at[h, rows_of(w, s_rows), :],
                    k_send.at[h, p], k_recv.at[h, w], p)

    def o_copy(h, p, w):
        return push(out_all.at[h, rows_of(p, t_rows), :], to.at[:, cols_of(w, h)],
                    o_send.at[h, p], o_recv.at[h, w], p)

    def g_copy(h, p, w):
        return push(sg_all.at[h, rows_of(p, s_rows), :], sg.at[:, cols_of(w, h)],
                    g_send.at[h, p], g_recv.at[h, w], p)

    def own_in(h):
        return (
            pltpu.make_async_copy(qg.at[:, cols_of(me, h)], qd_all.at[h, rows_of(me, t_rows), :], own.at[0, h]),
            pltpu.make_async_copy(kvs.at[:, cols_of(me, h)], kv_all.at[h, rows_of(me, s_rows), :], own.at[1, h]),
        )

    def own_out(h):
        return (
            pltpu.make_async_copy(out_all.at[h, rows_of(me, t_rows), :], to.at[:, cols_of(me, h)], own.at[2, h]),
            pltpu.make_async_copy(sg_all.at[h, rows_of(me, s_rows), :], sg.at[:, cols_of(me, h)], own.at[3, h]),
        )

    def each(body):
        @pl.loop(1, n)
        def _(d):
            body(partner(d))

    barrier = pltpu.get_barrier_semaphore()
    each(lambda p: pl.semaphore_signal(
        barrier, inc=1, device_id={"section": p}, device_id_type=pl.DeviceIdType.MESH))

    @pl.loop(0, heads)
    def _(h):
        for c in own_in(h):
            c.start()

    pl.semaphore_wait(barrier, n - 1)

    @pl.loop(0, heads)
    def _(h):
        def send(p):
            q_copy(h, p, me).start()
            k_copy(h, p, me).start()
        each(send)

    @pl.loop(0, heads)
    def _(h):
        for c in own_in(h):
            c.wait()

        def arrive(p):
            q_copy(h, me, p).wait_recv()
            k_copy(h, me, p).wait_recv()
        each(arrive)

        attend(h, tile, step, qd_all, kv_all, out_all, sg_all, s_scr, dp_scr, acc)

        def send(p):
            g_copy(h, p, me).start()
            o_copy(h, p, me).start()
        each(send)
        for c in own_out(h):
            c.start()

    @pl.loop(0, heads)
    def _(h):
        for c in own_out(h):
            c.wait()

        def finish(p):
            q_copy(h, p, me).wait_send()
            k_copy(h, p, me).wait_send()
            o_copy(h, p, me).wait_send()
            g_copy(h, p, me).wait_send()
            o_copy(h, me, p).wait_recv()
            g_copy(h, me, p).wait_recv()
        each(finish)


def solution(mesh):
    n = mesh.shape["section"]

    def per_device(query_grads, key_vals):
        t_rows, columns = query_grads.shape
        s_rows = key_vals.shape[0]
        heads = columns // (PAIR * n)
        targets, sources = t_rows * n, s_rows * n
        tile = math.gcd(targets, 256)
        step = max(math.gcd(sources, 256), sources // 8)
        anywhere = pl.BlockSpec(memory_space=pl.ANY)
        sems = pltpu.SemaphoreType.DMA((heads, n))
        return pl.pallas_call(
            functools.partial(kernel, n, heads, tile, step),
            out_shape=(
                jax.ShapeDtypeStruct(query_grads.shape, jnp.bfloat16),
                jax.ShapeDtypeStruct(key_vals.shape, jnp.bfloat16),
            ),
            in_specs=[anywhere, anywhere],
            out_specs=(anywhere, anywhere),
            scratch_shapes=[
                pltpu.VMEM((heads, targets, PAIR), jnp.bfloat16),
                pltpu.VMEM((heads, sources, PAIR), jnp.bfloat16),
                pltpu.VMEM((heads, targets, PAIR), jnp.bfloat16),
                pltpu.VMEM((heads, sources, PAIR), jnp.bfloat16),
                pltpu.VMEM((sources, tile), jnp.float32),
                pltpu.VMEM((sources, tile), jnp.float32),
                pltpu.VMEM((sources if targets > tile else 8, PAIR), jnp.float32),
            ] + [sems] * 8 + [pltpu.SemaphoreType.DMA((4, heads))],
            compiler_params=pltpu.CompilerParams(
                collective_id=0, has_side_effects=True,
                vmem_limit_bytes=48 * 1024 * 1024,
            ),
            cost_estimate=pl.CostEstimate(
                flops=24 * targets * sources * PAIR * heads,
                bytes_accessed=4 * (targets + sources) * columns // n,
                transcendentals=targets * sources * heads,
            ),
            name="exchange_attention",
        )(query_grads, key_vals)

    return jax.shard_map(
        per_device,
        mesh=mesh,
        in_specs=(P(("groups", "section"), None), P(("groups", "section"), None)),
        out_specs=(P(("groups", "section"), None), P(("groups", "section"), None)),
        check_vma=False,
    )
```

```python
import functools
import math

import jax
import jax.numpy as jnp
from jax import lax
from jax.experimental import pallas as pl
from jax.experimental.pallas import tpu as pltpu
from jax.sharding import PartitionSpec as P

HEAD = 64
PAIR = 2 * HEAD


def dot(a, b, da, db):
    return lax.dot_general(
        a, b, (((da,), (db,)), ((), ())), preferred_element_type=jnp.float32
    )


def scan_scores(q, kv_head, rows_step, s_out, dp_out, stats):
    scale = HEAD ** (-0.5)
    tile = q.shape[0]
    steps = kv_head.shape[0] // rows_step
    first = lax.broadcasted_iota(jnp.int32, (rows_step, PAIR), 1) < HEAD
    zero = jnp.zeros((rows_step, PAIR), jnp.bfloat16)
    peak = jnp.full((8, tile), -jnp.inf, jnp.float32)
    for i in range(steps):
        rows = pl.ds(i * rows_step, rows_step)
        kv = kv_head[rows, :]
        s = dot(jnp.where(first, kv, zero), q, 1, 1) * scale
        s_out[rows, :] = s
        dp_out[rows, :] = dot(jnp.where(first, zero, kv), q, 1, 1)
        peak = jnp.maximum(peak, jnp.max(s.reshape(rows_step // 8, 8, tile), axis=0))
    peak = jnp.max(peak, axis=0, keepdims=True)
    total = jnp.zeros((8, tile), jnp.float32)
    mixed = jnp.zeros((8, tile), jnp.float32)
    for i in range(steps):
        rows = pl.ds(i * rows_step, rows_step)
        e = jnp.exp(s_out[rows, :] - peak)
        s_out[rows, :] = e
        total = total + jnp.sum(e.reshape(rows_step // 8, 8, tile), axis=0)
        mixed = mixed + jnp.sum((e * dp_out[rows, :]).reshape(rows_step // 8, 8, tile), axis=0)
    total = jnp.sum(total, axis=0, keepdims=True)
    mixed = jnp.sum(mixed, axis=0, keepdims=True)
    stats[...] = jnp.concatenate(
        [peak, total, mixed, jnp.zeros((5, tile), jnp.float32)], axis=0)


def merge(mine, other):
    peak = jnp.maximum(mine[0:1, :], other[0:1, :])
    here = jnp.exp(mine[0:1, :] - peak)
    there = jnp.exp(other[0:1, :] - peak)
    inverse = 1.0 / (mine[1:2, :] * here + other[1:2, :] * there)
    shift = (mine[2:3, :] * here + other[2:3, :] * there) * inverse
    return here * inverse, shift


def finish_head(t, several, weight, shift, q, kv_head, rows_step, e_in, dp_in, acc, sg_head):
    scale = HEAD ** (-0.5)
    tile = q.shape[0]
    steps = kv_head.shape[0] // rows_step
    first = lax.broadcasted_iota(jnp.int32, (rows_step, PAIR), 1) < HEAD
    zero = jnp.zeros((rows_step, PAIR), jnp.bfloat16)
    out = jnp.zeros((tile, PAIR), jnp.float32)
    for i in range(steps):
        rows = pl.ds(i * rows_step, rows_step)
        probs = e_in[rows, :] * weight
        probs_low = probs.astype(jnp.bfloat16)
        d_scores = (probs * (dp_in[rows, :] - shift) * scale).astype(jnp.bfloat16)
        kv = kv_head[rows, :]
        vk = jnp.concatenate([kv[:, HEAD:], kv[:, :HEAD]], axis=1)
        out = out + dot(probs_low, jnp.where(first, vk, zero), 0, 0)
        out = out + dot(d_scores, jnp.where(first, zero, vk), 0, 0)
        grads = jnp.where(first, dot(d_scores, q, 1, 0), dot(probs_low, q, 1, 0))
        if several:
            grads = jnp.where(t == 0, 0.0, acc[rows, :]) + grads
            acc[rows, :] = grads
        sg_head[rows, :] = grads.astype(jnp.bfloat16)
    return out


def kernel(
    n, heads, tile, step,
    qg, kvs, to, sg,
    qd_all, kv_all, out_all, sg_all, s_scr, dp_scr, acc, parts, stat_mine, stat_other,
    q_send, q_recv, k_send, k_recv, o_send, o_recv, g_send, g_recv, s_send, s_recv, own, own_q,
):
    me = lax.axis_index("section")
    t_rows = qg.shape[0]
    s_rows = kvs.shape[0]
    half = n // 2
    tiles = t_rows * n // tile
    items = heads * tiles
    side = me // half
    base = side * half
    place = lax.rem(me, half)
    twin = lax.rem(me + half, n)
    width = heads * PAIR

    def rows_of(p, rows):
        return pl.ds(pl.multiple_of(p * rows, rows), rows)

    def all_cols(p):
        return pl.ds(pl.multiple_of(lax.rem(p, half) * width, PAIR), width)

    def cols_of(p, h):
        return pl.ds(pl.multiple_of((lax.rem(p, half) * heads + h) * PAIR, PAIR), PAIR)

    def lanes(h):
        return pl.ds(pl.multiple_of(h * PAIR, PAIR), PAIR)

    def push(src, dst, send, recv, p):
        return pltpu.make_async_remote_copy(
            src_ref=src, dst_ref=dst, send_sem=send, recv_sem=recv,
            device_id={"section": p}, device_id_type=pl.DeviceIdType.MESH,
        )

    def q_copy(p, w):
        return push(qg.at[:, all_cols(p)], qd_all.at[rows_of(w, t_rows), :],
                    q_send.at[p], q_recv.at[w], p)

    def k_copy(h, p, w):
        return push(kvs.at[:, cols_of(p, h)], kv_all.at[h, rows_of(lax.rem(w, half), s_rows), :],
                    k_send.at[h, lax.rem(p, half)], k_recv.at[h, lax.rem(w, half)], p)

    def o_copy(h, p, w):
        return push(out_all.at[h, rows_of(p, t_rows), :], parts.at[w // half, :, cols_of(w, h)],
                    o_send.at[h, p], o_recv.at[h, w], p)

    def g_copy(h, p, w):
        return push(sg_all.at[h, rows_of(lax.rem(p, half), s_rows), :], sg.at[:, cols_of(w, h)],
                    g_send.at[h, lax.rem(p, half)], g_recv.at[h, lax.rem(w, half)], p)

    def stat_copy(i):
        return push(stat_mine.at[i], stat_other.at[i], s_send.at[i], s_recv.at[i], twin)

    def own_in(h):
        return pltpu.make_async_copy(
            kvs.at[:, cols_of(me, h)], kv_all.at[h, rows_of(place, s_rows), :], own.at[0, h])

    def own_query():
        return pltpu.make_async_copy(
            qg.at[:, all_cols(me)], qd_all.at[rows_of(me, t_rows), :], own_q.at[0])

    def own_out(h):
        return (
            pltpu.make_async_copy(out_all.at[h, rows_of(me, t_rows), :],
                                  parts.at[side, :, cols_of(me, h)], own.at[1, h]),
            pltpu.make_async_copy(sg_all.at[h, rows_of(place, s_rows), :],
                                  sg.at[:, cols_of(me, h)], own.at[2, h]),
        )

    def each(body):
        @pl.loop(1, n)
        def _(d):
            body(lax.rem(me + d, n))

    def near(body):
        @pl.loop(1, half)
        def _(d):
            body(base + lax.rem(place + d, half))

    barrier = pltpu.get_barrier_semaphore()
    each(lambda p: pl.semaphore_signal(
        barrier, inc=1, device_id={"section": p}, device_id_type=pl.DeviceIdType.MESH))
    own_query().start()

    @pl.loop(0, heads)
    def _(h):
        own_in(h).start()

    pl.semaphore_wait(barrier, n - 1)
    each(lambda p: q_copy(p, me).start())

    @pl.loop(0, heads)
    def _(h):
        near(lambda p: k_copy(h, p, me).start())

    own_query().wait()
    each(lambda p: q_copy(me, p).wait_recv())

    def query(h, t):
        return qd_all[pl.ds(pl.multiple_of(t * tile, tile), tile), lanes(h)]

    @pl.loop(0, items + 1)
    def _(i):
        @pl.when(i < items)
        def _():
            h, t = i // tiles, lax.rem(i, tiles)
            slot = lax.rem(i, 2)

            @pl.when(t == 0)
            def _():
                own_in(h).wait()
                near(lambda p: k_copy(h, me, p).wait_recv())

            scan_scores(query(h, t), kv_all.at[h], step, s_scr.at[slot], dp_scr.at[slot],
                        stat_mine.at[i])
            stat_copy(i).start()

        @pl.when(i > 0)
        def _():
            j = i - 1
            h, t = j // tiles, lax.rem(j, tiles)
            slot = lax.rem(j, 2)
            stat_copy(j).wait_recv()
            weight, shift = merge(stat_mine[j], stat_other[j])
            out_all[h, pl.ds(pl.multiple_of(t * tile, tile), tile), :] = finish_head(
                t, tiles > 1, weight, shift, query(h, t), kv_all.at[h], step,
                s_scr.at[slot], dp_scr.at[slot], acc, sg_all.at[h])

            @pl.when(t == tiles - 1)
            def _():
                near(lambda p: g_copy(h, p, me).start())
                each(lambda p: o_copy(h, p, me).start())
                for c in own_out(h):
                    c.start()

    each(lambda p: q_copy(p, me).wait_send())

    @pl.loop(0, items)
    def _(i):
        stat_copy(i).wait_send()

    @pl.loop(0, heads)
    def _(h):
        for c in own_out(h):
            c.wait()

        def far(p):
            o_copy(h, p, me).wait_send()
            o_copy(h, me, p).wait_recv()
        each(far)

    to[...] = (parts[0] + parts[1]).astype(jnp.bfloat16)

    @pl.loop(0, heads)
    def _(h):
        def close(p):
            k_copy(h, p, me).wait_send()
            g_copy(h, p, me).wait_send()
            g_copy(h, me, p).wait_recv()
        near(close)


def solution(mesh):
    n = mesh.shape["section"]
    half = n // 2

    def per_device(query_grads, key_vals):
        t_rows, columns = query_grads.shape
        s_rows = key_vals.shape[0]
        heads = columns // (PAIR * half)
        targets, sources = t_rows * n, s_rows * half
        tile = math.gcd(targets, 256)
        items = heads * (targets // tile)
        step = max(math.gcd(sources, 256), sources // 8)
        anywhere = pl.BlockSpec(memory_space=pl.ANY)
        dma = pltpu.SemaphoreType.DMA
        return pl.pallas_call(
            functools.partial(kernel, n, heads, tile, step),
            out_shape=(
                jax.ShapeDtypeStruct(query_grads.shape, jnp.bfloat16),
                jax.ShapeDtypeStruct(key_vals.shape, jnp.bfloat16),
            ),
            in_specs=[anywhere, anywhere],
            out_specs=(pl.BlockSpec(memory_space=pltpu.VMEM), anywhere),
            scratch_shapes=[
                pltpu.VMEM((targets, heads * PAIR), jnp.bfloat16),
                pltpu.VMEM((heads, sources, PAIR), jnp.bfloat16),
                pltpu.VMEM((heads, targets, PAIR), jnp.float32),
                pltpu.VMEM((heads, sources, PAIR), jnp.bfloat16),
                pltpu.VMEM((2, sources, tile), jnp.float32),
                pltpu.VMEM((2, sources, tile), jnp.float32),
                pltpu.VMEM((sources if targets > tile else 8, PAIR), jnp.float32),
                pltpu.VMEM((2, t_rows, columns), jnp.float32),
                pltpu.VMEM((items, 8, tile), jnp.float32),
                pltpu.VMEM((items, 8, tile), jnp.float32),
                dma((n,)), dma((n,)),
                dma((heads, half)), dma((heads, half)),
                dma((heads, n)), dma((heads, n)),
                dma((heads, half)), dma((heads, half)),
                dma((items,)), dma((items,)),
                dma((3, heads)), dma((1,)),
            ],
            compiler_params=pltpu.CompilerParams(
                collective_id=0, has_side_effects=True,
                vmem_limit_bytes=48 * 1024 * 1024,
            ),
            cost_estimate=pl.CostEstimate(
                flops=24 * targets * sources * PAIR * heads,
                bytes_accessed=4 * (targets + sources) * heads * PAIR,
                transcendentals=targets * sources * heads,
            ),
            name="exchange_attention",
        )(query_grads, key_vals)

    return jax.shard_map(
        per_device,
        mesh=mesh,
        in_specs=(P(("groups", "section"), None), P(("groups", "section"), None)),
        out_specs=(P(("groups", "section"), None), P(("groups", "section"), None)),
        check_vma=False,
    )
```

```python
import functools
import math

import jax
import jax.numpy as jnp
from jax import lax
from jax.experimental import pallas as pl
from jax.experimental.pallas import tpu as pltpu
from jax.sharding import PartitionSpec as P

HEAD = 64
PAIR = 2 * HEAD


def dot(a, b, da, db):
    return lax.dot_general(
        a, b, (((da,), (db,)), ((), ())), preferred_element_type=jnp.float32
    )


def scan_scores(q, kv_head, rows_step, s_out, dp_out, stats):
    scale = HEAD ** (-0.5)
    tile = q.shape[0]
    steps = kv_head.shape[0] // rows_step
    first = lax.broadcasted_iota(jnp.int32, (rows_step, PAIR), 1) < HEAD
    zero = jnp.zeros((rows_step, PAIR), jnp.bfloat16)
    peak = jnp.full((8, tile), -jnp.inf, jnp.float32)
    for i in range(steps):
        rows = pl.ds(i * rows_step, rows_step)
        kv = kv_head[rows, :]
        s = dot(jnp.where(first, kv, zero), q, 1, 1) * scale
        s_out[rows, :] = s
        dp_out[rows, :] = dot(jnp.where(first, zero, kv), q, 1, 1)
        peak = jnp.maximum(peak, jnp.max(s.reshape(rows_step // 8, 8, tile), axis=0))
    peak = jnp.max(peak, axis=0, keepdims=True)
    total = jnp.zeros((8, tile), jnp.float32)
    mixed = jnp.zeros((8, tile), jnp.float32)
    for i in range(steps):
        rows = pl.ds(i * rows_step, rows_step)
        e = jnp.exp(s_out[rows, :] - peak)
        s_out[rows, :] = e
        total = total + jnp.sum(e.reshape(rows_step // 8, 8, tile), axis=0)
        mixed = mixed + jnp.sum((e * dp_out[rows, :]).reshape(rows_step // 8, 8, tile), axis=0)
    total = jnp.sum(total, axis=0, keepdims=True)
    mixed = jnp.sum(mixed, axis=0, keepdims=True)
    stats[...] = jnp.concatenate(
        [peak, total, mixed, jnp.zeros((5, tile), jnp.float32)], axis=0)


def merge(mine, other):
    peak = jnp.maximum(mine[0:1, :], other[0:1, :])
    here = jnp.exp(mine[0:1, :] - peak)
    there = jnp.exp(other[0:1, :] - peak)
    inverse = 1.0 / (mine[1:2, :] * here + other[1:2, :] * there)
    shift = (mine[2:3, :] * here + other[2:3, :] * there) * inverse
    return here * inverse, shift


def finish_head(t, several, weight, shift, q, kv_head, rows_step, e_in, dp_in, acc, sg_head):
    scale = HEAD ** (-0.5)
    tile = q.shape[0]
    steps = kv_head.shape[0] // rows_step
    first = lax.broadcasted_iota(jnp.int32, (rows_step, PAIR), 1) < HEAD
    zero = jnp.zeros((rows_step, PAIR), jnp.bfloat16)
    out = jnp.zeros((tile, PAIR), jnp.float32)
    for i in range(steps):
        rows = pl.ds(i * rows_step, rows_step)
        probs = e_in[rows, :] * weight
        probs_low = probs.astype(jnp.bfloat16)
        d_scores = (probs * (dp_in[rows, :] - shift) * scale).astype(jnp.bfloat16)
        kv = kv_head[rows, :]
        vk = jnp.concatenate([kv[:, HEAD:], kv[:, :HEAD]], axis=1)
        out = out + dot(probs_low, jnp.where(first, vk, zero), 0, 0)
        out = out + dot(d_scores, jnp.where(first, zero, vk), 0, 0)
        grads = jnp.where(first, dot(d_scores, q, 1, 0), dot(probs_low, q, 1, 0))
        if several:
            grads = jnp.where(t == 0, 0.0, acc[rows, :]) + grads
            acc[rows, :] = grads
        sg_head[rows, :] = grads.astype(jnp.bfloat16)
    return out


def kernel(
    n, heads, tile, step,
    qg, kvs, to, sg,
    qd_all, kv_all, out_all, sg_all, s_scr, dp_scr, acc, parts, stat_mine, stat_other,
    q_send, q_recv, k_send, k_recv, o_send, o_recv, g_send, g_recv, s_send, s_recv, own, own_q,
):
    me = lax.axis_index("section")
    t_rows = qg.shape[0]
    s_rows = kvs.shape[0]
    half = n // 2
    tiles = t_rows * n // tile
    items = heads * tiles
    side = me // half
    base = side * half
    place = lax.rem(me, half)
    twin = lax.rem(me + half, n)
    width = heads * PAIR

    def rows_of(p, rows):
        return pl.ds(pl.multiple_of(p * rows, rows), rows)

    def all_cols(p):
        return pl.ds(pl.multiple_of(lax.rem(p, half) * width, PAIR), width)

    def cols_of(p, h):
        return pl.ds(pl.multiple_of((lax.rem(p, half) * heads + h) * PAIR, PAIR), PAIR)

    def lanes(h):
        return pl.ds(pl.multiple_of(h * PAIR, PAIR), PAIR)

    def push(src, dst, send, recv, p):
        return pltpu.make_async_remote_copy(
            src_ref=src, dst_ref=dst, send_sem=send, recv_sem=recv,
            device_id={"section": p}, device_id_type=pl.DeviceIdType.MESH,
        )

    def q_copy(p, w):
        return push(qg.at[:, all_cols(p)], qd_all.at[rows_of(w, t_rows), :],
                    q_send.at[p], q_recv.at[w], p)

    def k_copy(h, p, w):
        return push(kvs.at[:, cols_of(p, h)], kv_all.at[h, rows_of(lax.rem(w, half), s_rows), :],
                    k_send.at[h, lax.rem(p, half)], k_recv.at[h, lax.rem(w, half)], p)

    def o_copy(h, p, w):
        return push(out_all.at[h, rows_of(p, t_rows), :], parts.at[w // half, :, cols_of(w, h)],
                    o_send.at[h, p], o_recv.at[h, w], p)

    def g_copy(h, p, w):
        return push(sg_all.at[h, rows_of(lax.rem(p, half), s_rows), :], sg.at[:, cols_of(w, h)],
                    g_send.at[h, lax.rem(p, half)], g_recv.at[h, lax.rem(w, half)], p)

    def stat_copy(i):
        return push(stat_mine.at[i], stat_other.at[i], s_send.at[i], s_recv.at[i], twin)

    def own_in(h):
        return pltpu.make_async_copy(
            kvs.at[:, cols_of(me, h)], kv_all.at[h, rows_of(place, s_rows), :], own.at[0, h])

    def own_query():
        return pltpu.make_async_copy(
            qg.at[:, all_cols(me)], qd_all.at[rows_of(me, t_rows), :], own_q.at[0])

    def own_out(h):
        return (
            pltpu.make_async_copy(out_all.at[h, rows_of(me, t_rows), :],
                                  parts.at[side, :, cols_of(me, h)], own.at[1, h]),
            pltpu.make_async_copy(sg_all.at[h, rows_of(place, s_rows), :],
                                  sg.at[:, cols_of(me, h)], own.at[2, h]),
        )

    def each(body):
        @pl.loop(1, n)
        def _(d):
            body(lax.rem(me + d, n))

    def near(body):
        @pl.loop(1, half)
        def _(d):
            body(base + lax.rem(place + d, half))

    barrier = pltpu.get_barrier_semaphore()
    each(lambda p: pl.semaphore_signal(
        barrier, inc=1, device_id={"section": p}, device_id_type=pl.DeviceIdType.MESH))
    own_query().start()

    @pl.loop(0, heads)
    def _(h):
        own_in(h).start()

    pl.semaphore_wait(barrier, n - 1)
    each(lambda p: q_copy(p, me).start())

    @pl.loop(0, heads)
    def _(h):
        near(lambda p: k_copy(h, p, me).start())

    own_query().wait()
    each(lambda p: q_copy(me, p).wait_recv())

    def query(h, t):
        return qd_all[pl.ds(pl.multiple_of(t * tile, tile), tile), lanes(h)]

    @pl.loop(0, items + 1)
    def _(i):
        @pl.when(i < items)
        def _():
            h, t = i // tiles, lax.rem(i, tiles)
            slot = lax.rem(i, 2)

            @pl.when(t == 0)
            def _():
                own_in(h).wait()
                near(lambda p: k_copy(h, me, p).wait_recv())

            scan_scores(query(h, t), kv_all.at[h], step, s_scr.at[slot], dp_scr.at[slot],
                        stat_mine.at[i])
            stat_copy(i).start()

        @pl.when(i > 0)
        def _():
            j = i - 1
            h, t = j // tiles, lax.rem(j, tiles)
            slot = lax.rem(j, 2)
            stat_copy(j).wait_recv()
            weight, shift = merge(stat_mine[j], stat_other[j])
            out_all[h, pl.ds(pl.multiple_of(t * tile, tile), tile), :] = finish_head(
                t, tiles > 1, weight, shift, query(h, t), kv_all.at[h], step,
                s_scr.at[slot], dp_scr.at[slot], acc, sg_all.at[h])

            @pl.when(t == tiles - 1)
            def _():
                each(lambda p: o_copy(h, p, me).start())
                near(lambda p: g_copy(h, p, me).start())
                for c in own_out(h):
                    c.start()

    each(lambda p: q_copy(p, me).wait_send())

    @pl.loop(0, items)
    def _(i):
        stat_copy(i).wait_send()

    @pl.loop(0, heads)
    def _(h):
        for c in own_out(h):
            c.wait()

        def far(p):
            o_copy(h, p, me).wait_send()
            o_copy(h, me, p).wait_recv()
        each(far)

    to[...] = (parts[0] + parts[1]).astype(jnp.bfloat16)

    @pl.loop(0, heads)
    def _(h):
        def close(p):
            k_copy(h, p, me).wait_send()
            g_copy(h, p, me).wait_send()
            g_copy(h, me, p).wait_recv()
        near(close)


def solution(mesh):
    n = mesh.shape["section"]
    half = n // 2

    def per_device(query_grads, key_vals):
        t_rows, columns = query_grads.shape
        s_rows = key_vals.shape[0]
        heads = columns // (PAIR * half)
        targets, sources = t_rows * n, s_rows * half
        tile = math.gcd(targets, 256)
        items = heads * (targets // tile)
        step = max(math.gcd(sources, 256), sources // 8)
        anywhere = pl.BlockSpec(memory_space=pl.ANY)
        dma = pltpu.SemaphoreType.DMA
        return pl.pallas_call(
            functools.partial(kernel, n, heads, tile, step),
            out_shape=(
                jax.ShapeDtypeStruct(query_grads.shape, jnp.bfloat16),
                jax.ShapeDtypeStruct(key_vals.shape, jnp.bfloat16),
            ),
            in_specs=[anywhere, anywhere],
            out_specs=(pl.BlockSpec(memory_space=pltpu.VMEM), anywhere),
            scratch_shapes=[
                pltpu.VMEM((targets, heads * PAIR), jnp.bfloat16),
                pltpu.VMEM((heads, sources, PAIR), jnp.bfloat16),
                pltpu.VMEM((heads, targets, PAIR), jnp.float32),
                pltpu.VMEM((heads, sources, PAIR), jnp.bfloat16),
                pltpu.VMEM((2, sources, tile), jnp.float32),
                pltpu.VMEM((2, sources, tile), jnp.float32),
                pltpu.VMEM((sources if targets > tile else 8, PAIR), jnp.float32),
                pltpu.VMEM((2, t_rows, columns), jnp.float32),
                pltpu.VMEM((items, 8, tile), jnp.float32),
                pltpu.VMEM((items, 8, tile), jnp.float32),
                dma((n,)), dma((n,)),
                dma((heads, half)), dma((heads, half)),
                dma((heads, n)), dma((heads, n)),
                dma((heads, half)), dma((heads, half)),
                dma((items,)), dma((items,)),
                dma((3, heads)), dma((1,)),
            ],
            compiler_params=pltpu.CompilerParams(
                collective_id=0, has_side_effects=True,
                vmem_limit_bytes=48 * 1024 * 1024,
            ),
            cost_estimate=pl.CostEstimate(
                flops=24 * targets * sources * PAIR * heads,
                bytes_accessed=4 * (targets + sources) * heads * PAIR,
                transcendentals=targets * sources * heads,
            ),
            name="exchange_attention",
        )(query_grads, key_vals)

    return jax.shard_map(
        per_device,
        mesh=mesh,
        in_specs=(P(("groups", "section"), None), P(("groups", "section"), None)),
        out_specs=(P(("groups", "section"), None), P(("groups", "section"), None)),
        check_vma=False,
    )
```
